512 devices in a mesh: occ: 32 (over x, z), vir: 16 (over y, core).
Axes of the slice: x: 4, y: 8, z: 8, core: 2. Of those that a mesh axis runs over, the one named last changes fastest.
Arguments:
- pair_integrals: bfloat16 [25600, 1536], P(('vir', 'occ')), may hold values from -0.4375 to 0.4375
- amplitudes: bfloat16 [1536, 40000], P('vir', 'occ'), may hold values from -6 to 6
- vir_irrep: int32 [2, 80], replicated, may hold values from 0 to 7, never falling along the last dimension, each value on 1 to 20 neighbouring positions
- occ_irrep: int32 [200], replicated, may hold values from 0 to 7, never falling along the last dimension, each value on 1 to 50 neighbouring positions
- pair_irrep: int32 [1536], replicated, may hold values from 0 to 7, never falling along the last dimension, each value on 1 to 768 neighbouring positions
- vir_energy: float32 [160], replicated, may hold values from 0.2 to 2
- occ_energy: float32 [200], replicated, may hold values from -1.5 to -0.3
Outputs:
- update: bfloat16 [25600, 40000], P('vir', 'occ')
The draws below stay inside these ranges and needn't reach their ends.
Inputs may be any that keep to these rules, and one draw needn't show every extreme that they name: `vir_irrep`: labels never fall along a slab; every label 0 to 7 occurs in each slab. `occ_irrep`: labels never fall; every label 0 to 7 occurs. `pair_irrep`: labels never fall; every label 0 to 7 occurs.
All inputs are finite; a program needn't handle non-finite values.
Results may differ from the reference program's by a relative error of at most 0.005.
Values may be sent and summed in bfloat16 or wider, within the bound.
No kernel may reach another device: no remote copies, remote signals or barrier semaphores. Data moves between devices by JAX's collectives and lax.ppermute only.
A program may use at most 128 MiB of HBM per device.

```python
import math
import jax
import jax.numpy as jnp
import numpy as np
from jax import lax

SLAB = 80
NW = 160
NOCC = 200
CD = 1536
AB = 25600
IJ = 40000


def levels(rng, extent, shards, low, high):
    def one(dim, blocks):
        draws = jax.random.uniform(jax.random.fold_in(jax.random.fold_in(rng, 6), dim), (blocks,), jnp.float32, low / len(shards), high / len(shards))
        return jnp.repeat(jnp.exp(draws), extent[dim] // blocks).reshape((-1,) + (1,) * (len(extent) - dim - 1))

    loudness = one(*shards[0])
    for cut in shards[1:]:
        loudness = loudness * one(*cut)
    return loudness


def length_profile(count, total, most, skew):
    portions = [(1 << 20) // math.isqrt(grade ** skew) + 1 for grade in range(2, count + 1)]
    rest, given = total - most - (count - 1), [1] * (count - 1)
    while rest > 0:
        free = [i for i in range(count - 1) if given[i] < most]
        whole, remaining = sum([portions[i] for i in free]), rest
        for i in free:
            more = min(most - given[i], max(1, remaining * portions[i] // whole), rest)
            given[i] = given[i] + more
            rest = rest - more
    return np.array([most] + given)


def ragged_sizes(stream_key, amount, total, bound, skew):
    if amount == 2:
        one = jax.random.randint(stream_key, (), max(1, total - bound), min(bound, total - 1) + 1)
        return jnp.stack([one, total - one])
    sizes = jnp.asarray(length_profile(amount, total, bound, skew), jnp.int32)
    pairs = (amount - 1) // 2
    donor, taker = sizes[1:1 + 2 * pairs:2], sizes[2:2 + 2 * pairs:2]
    room = jnp.minimum(donor - 1, bound - taker)
    passed = jax.random.randint(jax.random.fold_in(stream_key, 1), (pairs,), 0, 1 << 20) % (room + 1)
    sizes = sizes.at[1:1 + 2 * pairs:2].set(donor - passed).at[2:2 + 2 * pairs:2].set(taker + passed)
    return sizes[jax.random.permutation(jax.random.fold_in(stream_key, 2), amount)]


def centred(rng, dims, width, reach, shards=(), kind=jnp.bfloat16):
    factor_of = levels(rng, dims, shards, -0.22, 0.18) if shards else 1.0
    array = jax.random.normal(rng, dims, jnp.float32) * width * factor_of
    return jnp.minimum(jnp.maximum(array, -reach), reach).astype(kind)


def setup_inputs(seed: int = 0) -> dict:
    streams_of = jax.random.split(jax.random.key(seed), 8)
    pair_integrals = centred(streams_of[0], (AB, CD), (CD // 8) ** -0.5, 0.4375, ((0, 512),))
    amplitudes = centred(streams_of[1], (CD, IJ), 1.0, 6.0, ((0, 16), (1, 32)))
    vir_irrep = jax.vmap(lambda own: jnp.searchsorted(jnp.cumsum(ragged_sizes(own, 8, SLAB, SLAB // 4, 2)), jnp.arange(SLAB), side="right"))(jax.random.split(streams_of[2], 2)).reshape((2, SLAB)).astype(jnp.int32)
    occ_irrep = jnp.searchsorted(jnp.cumsum(ragged_sizes(streams_of[3], 8, NOCC, NOCC // 4, 2)), jnp.arange(NOCC), side="right").astype(jnp.int32)
    pair_irrep = jnp.searchsorted(jnp.cumsum(ragged_sizes(streams_of[4], 8, CD, CD // 2, 2)), jnp.arange(CD), side="right").astype(jnp.int32)
    vir_energy = jnp.clip(jax.random.uniform(streams_of[5], (NW,), jnp.float32, 0.2, 2.0), 0.2, 2.0)
    occ_energy = jnp.clip(jax.random.uniform(streams_of[6], (NOCC,), jnp.float32, -1.5, -0.3), -1.5, -0.3)
    return dict(pair_integrals=pair_integrals, amplitudes=amplitudes, vir_irrep=vir_irrep, occ_irrep=occ_irrep, pair_irrep=pair_irrep, vir_energy=vir_energy, occ_energy=occ_energy)


def reference(pair_integrals, amplitudes, vir_irrep, occ_irrep, pair_irrep, vir_energy, occ_energy):
    vir_count = vir_energy.shape[0]
    labels_vir = vir_irrep.reshape(-1)
    label_ij = jnp.bitwise_xor(occ_irrep[:, None], occ_irrep[None, :]).reshape(-1)
    energy_ij = (occ_energy[:, None] + occ_energy[None, :]).reshape(-1)
    integral_cube = pair_integrals.reshape(vir_count, vir_count, -1)

    def one_first(index):
        label_ab = jnp.bitwise_xor(labels_vir[index], labels_vir)
        masked_rows = jnp.where(label_ab[:, None] == pair_irrep[None, :], integral_cube[index], jnp.zeros((), pair_integrals.dtype))
        product = jnp.dot(masked_rows, amplitudes, preferred_element_type=jnp.float32)
        return jnp.where(label_ab[:, None] == label_ij[None, :], product, jnp.zeros((), jnp.float32)).astype(jnp.bfloat16)

    ladder = lax.map(one_first, jnp.arange(vir_count, dtype=jnp.int32))

    def one_update(index):
        own_part = ladder[index].astype(jnp.float32)
        mirror_part = ladder[:, index].astype(jnp.float32)
        denominator = energy_ij[None, :] - (vir_energy[index] + vir_energy)[:, None]
        return ((own_part - mirror_part) / denominator).astype(jnp.bfloat16)

    update = lax.map(one_update, jnp.arange(vir_count, dtype=jnp.int32))
    return update.reshape(vir_count * vir_count, -1)
```

```python
import functools

import jax
import jax.numpy as jnp
import numpy as np
from jax import lax
from jax.experimental import pallas as pl
from jax.experimental.pallas import tpu as pltpu
from jax.sharding import PartitionSpec as P

SLAB = 80
NW = 160
NOCC = 200
CD = 1536
PAIRS = 1250
OWN = 10
ROWS = 50
CDS = 48
SLOTS = 384
LANES = 128
F32 = jnp.float32
BF16 = jnp.bfloat16
VMEM = pl.BlockSpec(memory_space=pltpu.VMEM)


def params():
    return pltpu.CompilerParams(vmem_limit_bytes=48 * 1024 * 1024)


def call(kernel, shapes, args):
    specs = jax.tree.map(lambda _: VMEM, shapes)
    return pl.pallas_call(
        kernel, out_shape=shapes, in_specs=[VMEM] * len(args), out_specs=specs, compiler_params=params()
    )(*args)


def dot(left, right, contract=((1,), (0,))):
    return lax.dot_general(left, right, (contract, ((), ())), preferred_element_type=F32)


def lookup(indices, table):
    chosen = indices[:, None] == jnp.arange(table.shape[0], dtype=jnp.int32)[None, :]
    return jnp.sum(jnp.where(chosen, table[None, :], jnp.zeros((), table.dtype)), axis=1)


def pack_columns(amp_ref, label_cd_ref, label_ij_ref, slot_ref, out_ref):
    keep = label_cd_ref[...] == label_ij_ref[...]
    masked = jnp.where(keep, amp_ref[...].astype(F32), 0.0).astype(BF16)
    rows = lax.broadcasted_iota(jnp.int32, (SLOTS, PAIRS), 0)
    place = jnp.where(rows == slot_ref[...], 1.0, 0.0).astype(BF16)
    out_ref[...] = dot(masked, place, ((1,), (1,))).astype(BF16)


def turn_rows(rows_ref, out_ref):
    row = lax.broadcasted_iota(jnp.int32, (ROWS, LANES), 0)
    lane = lax.broadcasted_iota(jnp.int32, (ROWS, LANES), 1)
    low = dot(rows_ref[...], jnp.where(lane == row, 1.0, 0.0).astype(BF16), ((0,), (0,)))
    high = dot(rows_ref[...], jnp.where(lane == row + 64, 1.0, 0.0).astype(BF16), ((0,), (0,)))
    half = CDS // 2
    for dest in range(CD // CDS):
        at = dest * CDS
        out_ref[dest] = (low[at : at + half] + high[at + half : at + CDS]).astype(BF16)


def by_partner(got_ref, out_ref):
    half = CDS // 2
    lane = lax.broadcasted_iota(jnp.int32, (half, LANES), 1)
    inside = [(lane >= OWN * a) & (lane < OWN * (a + 1)) for a in range(OWN)]
    for partner in range(16):
        halves = []
        for h in range(2):
            block = jnp.zeros((half, LANES), F32)
            for a in range(OWN):
                granule = a * 16 + partner
                source, piece = granule // 5, granule % 5
                shift = (OWN * a - 64 * h - OWN * piece) % LANES
                moved = got_ref[source].astype(F32)
                if shift:
                    moved = pltpu.roll(moved, shift, axis=1)
                block = jnp.where(inside[a], moved, block)
            halves.append(block)
        out_ref[partner] = jnp.concatenate(halves, axis=0).astype(BF16)


def difference(own_ref, mirror_ref, swap_ref, label_ab_ref, label_cd_ref, out_ref):
    label_cd = label_cd_ref[...]
    for slab in range(2):
        for odd in range(2):
            packed = jnp.zeros((CDS, LANES), F32)
            for quarter in range(4):
                partner = 8 * slab + 2 * quarter + odd
                mirrored = dot(mirror_ref[partner], swap_ref[...])
                diff = own_ref[partner].astype(F32) - mirrored
                keep = label_ab_ref[partner : partner + 1, :] == label_cd
                packed = jnp.where(keep, diff, packed)
            packed = packed.astype(BF16)
            for copy in range(8):
                out_ref[copy, 2 * slab + odd] = packed


def turn_back(got_ref, place_ref, out_ref):
    total = jnp.zeros((400, 384), F32)
    for part in range(4):
        block = got_ref[:, part].reshape(384, LANES)
        total = total + dot(place_ref[part], block, ((1,), (1,)))
    for a in range(OWN):
        rows = total[40 * a : 40 * a + 40].astype(BF16)
        for copy in range(4):
            out_ref[copy, a] = rows


def finish(packed_ref, amp_ref, spread_ref, label_ab_ref, label_cd_ref, energy_ab_ref, label_ij_ref, energy_ij_ref,
           slot_ref, out_ref, place_ref):
    @pl.when(pl.program_id(0) == 0)
    def _():
        rows = lax.broadcasted_iota(jnp.int32, (SLOTS, PAIRS), 0)
        place_ref[...] = jnp.where(rows == slot_ref[...], 1.0, 0.0).astype(BF16)

    label_ab = label_ab_ref[0]
    total = jnp.zeros((NW, SLOTS), F32)
    for part in range(4):
        at = 384 * part
        spread = dot(spread_ref[...], packed_ref[part, 0])
        keep = label_ab == label_cd_ref[:, at : at + 384]
        masked = jnp.where(keep, spread, 0.0).astype(BF16)
        total = total + dot(masked, amp_ref[at : at + 384, :])
    ladder = dot(total.astype(BF16), place_ref[...])
    update = ladder / (energy_ij_ref[...] - energy_ab_ref[0])
    out_ref[...] = jnp.where(label_ab == label_ij_ref[...], update, 0.0).astype(BF16)


def swap_table():
    table = np.zeros((LANES, LANES), np.float32)
    for a in range(OWN):
        for b in range(OWN):
            table[b * OWN + a, a * OWN + b] = 1.0
    return table


def place_table():
    table = np.zeros((4, 400, LANES), np.float32)
    for a in range(OWN):
        for part in range(4):
            for b in range(OWN):
                table[part, a * 40 + part * OWN + b, a * OWN + b] = 1.0
    return table


def spread_table():
    table = np.zeros((NW, 40), np.float32)
    for b in range(NW):
        slab, within = b // SLAB, b % SLAB
        table[b, slab * 20 + within % 20] = 1.0
    return table


def on_device(pair_integrals, amplitudes, vir_irrep, occ_irrep, pair_irrep, vir_energy, occ_energy):
    occ = lax.axis_index("occ")
    vir = lax.axis_index("vir")
    z_groups = [[8 * x + z for z in range(8)] for x in range(4)]
    x_groups = [[8 * x + z for x in range(4)] for z in range(8)]

    labels_vir = vir_irrep.reshape(-1)
    own_labels = lax.dynamic_slice_in_dim(labels_vir, vir * OWN, OWN)
    own_energy = lax.dynamic_slice_in_dim(vir_energy, vir * OWN, OWN)
    label_ab = jnp.bitwise_xor(own_labels[:, None], labels_vir[None, :])
    energy_ab = own_energy[:, None] + vir_energy[None, :]
    occ_pair = occ * PAIRS + jnp.arange(PAIRS, dtype=jnp.int32)
    first_occ = occ_pair // NOCC
    second_occ = occ_pair % NOCC
    label_ij = jnp.bitwise_xor(lookup(first_occ, occ_irrep), lookup(second_occ, occ_irrep))[None, :]
    energy_ij = (lookup(first_occ, occ_energy) + lookup(second_occ, occ_energy))[None, :]
    slot = ((first_occ - (occ * PAIRS) // NOCC) * 50 + second_occ % 50)[None, :]

    label_rows = lax.dynamic_slice_in_dim(pair_irrep, vir * 96, 96)[:, None]
    packed_amp = call(
        pack_columns, jax.ShapeDtypeStruct((96, SLOTS), BF16), (amplitudes, label_rows, label_ij, slot)
    )
    all_amp = lax.all_gather(packed_amp, "vir", axis=0, tiled=True)

    turned = call(turn_rows, jax.ShapeDtypeStruct((32, CDS // 2, LANES), BF16), (pair_integrals,))
    slices = lax.all_to_all(turned, "occ", split_axis=0, concat_axis=0, tiled=True)
    blocks = call(by_partner, jax.ShapeDtypeStruct((16, CDS, LANES), BF16), (slices,))
    mirror = lax.all_to_all(blocks, "vir", split_axis=0, concat_axis=0, tiled=True)
    block_labels = label_ab.reshape(OWN, 16, OWN).transpose(1, 0, 2).reshape(16, OWN * OWN)
    block_labels = jnp.pad(block_labels, ((0, 0), (0, LANES - OWN * OWN)), constant_values=-1)
    label_cds = lax.dynamic_slice_in_dim(pair_irrep, occ * CDS, CDS)[:, None]
    copies = call(
        difference,
        jax.ShapeDtypeStruct((8, 4, CDS, LANES), BF16),
        (blocks, mirror, jnp.asarray(swap_table(), BF16), block_labels, label_cds),
    )
    line = lax.all_to_all(copies, "occ", split_axis=0, concat_axis=0, tiled=True, axis_index_groups=z_groups)
    rows = call(
        turn_back, jax.ShapeDtypeStruct((4, OWN, 40, 384), BF16), (line, jnp.asarray(place_table(), BF16))
    )
    packed = lax.all_to_all(rows, "occ", split_axis=0, concat_axis=0, tiled=True, axis_index_groups=x_groups)

    whole = lambda *shape: pl.BlockSpec(shape, lambda i: (0,) * len(shape))
    return pl.pallas_call(
        finish,
        grid=(OWN,),
        out_shape=jax.ShapeDtypeStruct((OWN * NW, PAIRS), BF16),
        in_specs=[
            pl.BlockSpec((4, 1, 40, 384), lambda i: (0, i, 0, 0)),
            whole(CD, SLOTS),
            whole(NW, 40),
            pl.BlockSpec((1, NW, 1), lambda i: (i, 0, 0)),
            whole(1, CD),
            pl.BlockSpec((1, NW, 1), lambda i: (i, 0, 0)),
            whole(1, PAIRS),
            whole(1, PAIRS),
            whole(1, PAIRS),
        ],
        out_specs=pl.BlockSpec((NW, PAIRS), lambda i: (i, 0)),
        scratch_shapes=[pltpu.VMEM((SLOTS, PAIRS), BF16)],
        compiler_params=params(),
    )(
        packed,
        all_amp,
        jnp.asarray(spread_table(), BF16),
        label_ab[:, :, None],
        pair_irrep[None, :],
        energy_ab[:, :, None],
        label_ij,
        energy_ij,
        slot,
    )


def solution(mesh):
    in_specs = (P(("vir", "occ"), None), P("vir", "occ"), P(), P(), P(), P(), P())
    out_specs = P("vir", "occ")
    return jax.shard_map(
        on_device, mesh=mesh, in_specs=in_specs, out_specs=out_specs, check_vma=False
    )
```

```python
import jax
import jax.numpy as jnp
import numpy as np
from jax import lax
from jax.experimental import pallas as pl
from jax.experimental.pallas import tpu as pltpu
from jax.sharding import PartitionSpec as P

SLAB = 80
NW = 160
NOCC = 200
CD = 1536
PAIRS = 1250
OWN = 10
ROWS = 50
CDS = 48
SLOTS = 384
LANES = 128
STEP = 5
CHIPS = (0, 3, 5, 1, 4, 6, 7, 2)
F32 = jnp.float32
BF16 = jnp.bfloat16
VMEM = pl.BlockSpec(memory_space=pltpu.VMEM)


def params():
    return pltpu.CompilerParams(vmem_limit_bytes=48 * 1024 * 1024)


def call(kernel, shapes, args):
    specs = jax.tree.map(lambda _: VMEM, shapes)
    return pl.pallas_call(
        kernel, out_shape=shapes, in_specs=[VMEM] * len(args), out_specs=specs, compiler_params=params()
    )(*args)


def dot(left, right, contract=((1,), (0,))):
    return lax.dot_general(left, right, (contract, ((), ())), preferred_element_type=F32)


def lookup(indices, table):
    chosen = indices[:, None] == jnp.arange(table.shape[0], dtype=jnp.int32)[None, :]
    return jnp.sum(jnp.where(chosen, table[None, :], jnp.zeros((), table.dtype)), axis=1)


def pack_columns(amp_ref, label_cd_ref, label_ij_ref, slot_ref, out_ref):
    keep = label_cd_ref[...] == label_ij_ref[...]
    masked = jnp.where(keep, amp_ref[...].astype(F32), 0.0).astype(BF16)
    rows = lax.broadcasted_iota(jnp.int32, (SLOTS, PAIRS), 0)
    place = jnp.where(rows == slot_ref[...], 1.0, 0.0).astype(BF16)
    out_ref[0] = dot(masked, place, ((1,), (1,))).astype(BF16)


def turn_rows(rows_ref, out_ref):
    row = lax.broadcasted_iota(jnp.int32, (ROWS, LANES), 0)
    lane = lax.broadcasted_iota(jnp.int32, (ROWS, LANES), 1)
    low = dot(rows_ref[...], jnp.where(lane == row, 1.0, 0.0).astype(BF16), ((0,), (0,)))
    high = dot(rows_ref[...], jnp.where(lane == row + 64, 1.0, 0.0).astype(BF16), ((0,), (0,)))
    half = CDS // 2
    for dest in range(CD // CDS):
        at = dest * CDS
        out_ref[dest] = (low[at : at + half] + high[at + half : at + CDS]).astype(BF16)


def by_partner(got_ref, out_ref):
    half = CDS // 2
    lane = lax.broadcasted_iota(jnp.int32, (half, LANES), 1)
    inside = [(lane >= OWN * a) & (lane < OWN * (a + 1)) for a in range(OWN)]
    for partner in range(16):
        halves = []
        for h in range(2):
            block = jnp.zeros((half, LANES), F32)
            for a in range(OWN):
                granule = a * 16 + partner
                source, piece = granule // 5, granule % 5
                shift = (OWN * a - 64 * h - OWN * piece) % LANES
                moved = got_ref[source].astype(F32)
                if shift:
                    moved = pltpu.roll(moved, shift, axis=1)
                block = jnp.where(inside[a], moved, block)
            halves.append(block)
        out_ref[partner] = jnp.concatenate(halves, axis=0).astype(BF16)


def difference(own_ref, mirror_ref, swap_ref, label_ab_ref, label_cd_ref, out_ref):
    label_cd = label_cd_ref[...]
    for slab in range(2):
        for odd in range(2):
            packed = jnp.zeros((CDS, LANES), F32)
            for quarter in range(4):
                partner = 8 * slab + 2 * quarter + odd
                mirrored = dot(mirror_ref[partner], swap_ref[...])
                diff = own_ref[partner].astype(F32) - mirrored
                keep = label_ab_ref[partner : partner + 1, :] == label_cd
                packed = jnp.where(keep, diff, packed)
            packed = packed.astype(BF16)
            for copy in range(8):
                out_ref[copy, 2 * slab + odd] = packed


def turn_back(got_ref, place_ref, out_ref):
    total = jnp.zeros((400, 384), F32)
    for part in range(4):
        block = got_ref[:, part].reshape(384, LANES)
        total = total + dot(place_ref[part], block, ((1,), (1,)))
    for a in range(OWN):
        rows = total[40 * a : 40 * a + 40].astype(BF16)
        for copy in range(4):
            out_ref[copy, a] = rows


def finish(packed_ref, three_ref, five_ref, core_three_ref, core_five_ref, pick_ref, vir_ref, own_label_ref, own_energy_ref, label_b_ref,
           spread_label_b_ref, energy_b_ref, label_cd_ref, label_ij_ref, energy_ij_ref, slot_ref, out_ref,
           amp_ref, place_ref, left_ref):
    step = pl.program_id(0)

    @pl.when(step == 0)
    def _():
        rows = lax.broadcasted_iota(jnp.int32, (SLOTS, PAIRS), 0)
        place_ref[...] = jnp.where(rows == slot_ref[...], 1.0, 0.0).astype(BF16)
        for part, core, first in ((three_ref, 0, 0), (five_ref, 0, 3), (core_three_ref, 1, 0), (core_five_ref, 1, 3)):
            for index in range(part.shape[0]):
                source = ((vir_ref[0] ^ core) + 2 * CHIPS[first + index]) & 15
                amp_ref[pl.ds(pl.multiple_of(96 * source, 96), 96), :] = part[index]

    for a in range(STEP):
        label_a = own_label_ref[step * STEP + a]
        for part in range(4):
            wanted = label_cd_ref[:, 384 * part : 384 * part + 384] ^ label_a
            values = packed_ref[part, a].astype(F32)
            values = jnp.concatenate([values, jnp.zeros((8, 384), F32)], axis=0)
            for quarter in range(4):
                keep = spread_label_b_ref[48 * quarter : 48 * quarter + 48, :] == wanted
                at = 192 * a + 48 * quarter
                left_ref[at : at + 48, 384 * part : 384 * part + 384] = jnp.where(keep, values, 0.0).astype(BF16)
    total = dot(left_ref[...], amp_ref[...]).astype(BF16)
    for a in range(STEP):
        picked = dot(pick_ref[...], total[192 * a : 192 * a + 192]).astype(BF16)
        ladder = dot(picked, place_ref[...])
        label_a = own_label_ref[step * STEP + a]
        energy_a = own_energy_ref[step * STEP + a]
        update = ladder / ((energy_ij_ref[...] - energy_a) - energy_b_ref[...])
        keep = label_b_ref[...] == (label_ij_ref[...] ^ label_a)
        out_ref[NW * a : NW * a + NW, :] = jnp.where(keep, update, 0.0).astype(BF16)


def swap_table():
    table = np.zeros((LANES, LANES), np.float32)
    for a in range(OWN):
        for b in range(OWN):
            table[b * OWN + a, a * OWN + b] = 1.0
    return table


def place_table():
    table = np.zeros((4, 400, LANES), np.float32)
    for a in range(OWN):
        for part in range(4):
            for b in range(OWN):
                table[part, a * 40 + part * OWN + b, a * OWN + b] = 1.0
    return table


def pick_table():
    table = np.zeros((NW, 192), np.float32)
    for b in range(NW):
        slab, within = b // SLAB, b % SLAB
        table[b, 48 * (within // 20) + 20 * slab + within % 20] = 1.0
    return table


def on_device(pair_integrals, amplitudes, vir_irrep, occ_irrep, pair_irrep, vir_energy, occ_energy):
    occ = lax.axis_index("occ")
    vir = lax.axis_index("vir")
    z_groups = [[8 * x + z for z in range(8)] for x in range(4)]
    x_groups = [[8 * x + z for x in range(4)] for z in range(8)]

    labels_vir = vir_irrep.reshape(-1)
    own_labels = lax.dynamic_slice_in_dim(labels_vir, vir * OWN, OWN)
    own_energy = lax.dynamic_slice_in_dim(vir_energy, vir * OWN, OWN)
    label_ab = jnp.bitwise_xor(own_labels[:, None], labels_vir[None, :])
    occ_pair = occ * PAIRS + jnp.arange(PAIRS, dtype=jnp.int32)
    first_occ = occ_pair // NOCC
    second_occ = occ_pair % NOCC
    label_ij = jnp.bitwise_xor(lookup(first_occ, occ_irrep), lookup(second_occ, occ_irrep))[None, :]
    energy_ij = (lookup(first_occ, occ_energy) + lookup(second_occ, occ_energy))[None, :]
    slot = ((first_occ - (occ * PAIRS) // NOCC) * 50 + second_occ % 50)[None, :]

    label_rows = lax.dynamic_slice_in_dim(pair_irrep, vir * 96, 96)[:, None]
    packed_amp = call(
        pack_columns, jax.ShapeDtypeStruct((1, 96, SLOTS), BF16), (amplitudes, label_rows, label_ij, slot)
    )

    from_chip = lambda array, k: lax.ppermute(array, "vir", [(i, (i - 2 * k) % 16) for i in range(16)])

    turned = call(turn_rows, jax.ShapeDtypeStruct((32, CDS // 2, LANES), BF16), (pair_integrals,))
    slices = lax.all_to_all(turned, "occ", split_axis=0, concat_axis=0, tiled=True)
    blocks = call(by_partner, jax.ShapeDtypeStruct((16, CDS, LANES), BF16), (slices,))
    mirror = lax.all_to_all(blocks, "vir", split_axis=0, concat_axis=0, tiled=True)
    block_labels = label_ab.reshape(OWN, 16, OWN).transpose(1, 0, 2).reshape(16, OWN * OWN)
    block_labels = jnp.pad(block_labels, ((0, 0), (0, LANES - OWN * OWN)), constant_values=-1)
    label_cds = lax.dynamic_slice_in_dim(pair_irrep, occ * CDS, CDS)[:, None]
    copies = call(
        difference,
        jax.ShapeDtypeStruct((8, 4, CDS, LANES), BF16),
        (blocks, mirror, jnp.asarray(swap_table(), BF16), block_labels, label_cds),
    )
    copies, packed_amp = lax.optimization_barrier((copies, packed_amp))
    amp_three = jnp.concatenate([packed_amp, from_chip(packed_amp, 3), from_chip(packed_amp, 5)], axis=0)
    line = lax.all_to_all(copies, "occ", split_axis=0, concat_axis=0, tiled=True, axis_index_groups=z_groups)
    rows = call(
        turn_back, jax.ShapeDtypeStruct((4, OWN, 40, 384), BF16), (line, jnp.asarray(place_table(), BF16))
    )
    rows, amp_three = lax.optimization_barrier((rows, amp_three))
    from_core = lambda array: lax.ppermute(array, "vir", [(i, i ^ 1) for i in range(16)])
    amp_five = jnp.concatenate([from_chip(amp_three, 1), from_chip(amp_three[:2], 7)], axis=0)
    amp_parts = (amp_three, amp_five, from_core(amp_three), from_core(amp_five))
    packed = lax.all_to_all(rows, "occ", split_axis=0, concat_axis=0, tiled=True, axis_index_groups=x_groups)

    spread_labels = jnp.pad(
        labels_vir.reshape(2, 4, 20).transpose(1, 0, 2).reshape(4, 40), ((0, 0), (0, 8)), constant_values=-1
    ).reshape(192, 1)
    whole = lambda *shape: pl.BlockSpec(shape, lambda i: (0,) * len(shape))
    scalars = pl.BlockSpec(memory_space=pltpu.SMEM)
    return pl.pallas_call(
        finish,
        grid=(OWN // STEP,),
        out_shape=jax.ShapeDtypeStruct((OWN * NW, PAIRS), BF16),
        in_specs=[
            pl.BlockSpec((4, STEP, 40, 384), lambda i: (0, i, 0, 0)),
            whole(3, 96, SLOTS),
            whole(5, 96, SLOTS),
            whole(3, 96, SLOTS),
            whole(5, 96, SLOTS),
            whole(NW, 192),
            scalars,
            scalars,
            scalars,
            whole(NW, 1),
            whole(192, 1),
            whole(NW, 1),
            whole(1, CD),
            whole(1, PAIRS),
            whole(1, PAIRS),
            whole(1, PAIRS),
        ],
        out_specs=pl.BlockSpec((STEP * NW, PAIRS), lambda i: (i, 0)),
        scratch_shapes=[
            pltpu.VMEM((CD, SLOTS), BF16),
            pltpu.VMEM((SLOTS, PAIRS), BF16),
            pltpu.VMEM((STEP * 192, CD), BF16),
        ],
        compiler_params=params(),
    )(
        packed,
        *amp_parts,
        jnp.asarray(pick_table(), BF16),
        vir.reshape(1),
        own_labels,
        own_energy,
        labels_vir[:, None],
        spread_labels,
        vir_energy[:, None],
        pair_irrep[None, :],
        label_ij,
        energy_ij,
        slot,
    )


def solution(mesh):
    in_specs = (P(("vir", "occ"), None), P("vir", "occ"), P(), P(), P(), P(), P())
    out_specs = P("vir", "occ")
    return jax.shard_map(
        on_device, mesh=mesh, in_specs=in_specs, out_specs=out_specs, check_vma=False
    )
```

```python
import jax
import jax.numpy as jnp
import numpy as np
from jax import lax
from jax.experimental import pallas as pl
from jax.experimental.pallas import tpu as pltpu
from jax.sharding import PartitionSpec as P

SLAB = 80
NW = 160
NOCC = 200
CD = 1536
PAIRS = 1250
OWN = 10
ROWS = 50
CDS = 48
SLOTS = 384
LANES = 128
STEP = 5
F32 = jnp.float32
BF16 = jnp.bfloat16
VMEM = pl.BlockSpec(memory_space=pltpu.VMEM)


def params():
    return pltpu.CompilerParams(vmem_limit_bytes=48 * 1024 * 1024)


def call(kernel, shapes, args):
    specs = jax.tree.map(lambda _: VMEM, shapes)
    return pl.pallas_call(
        kernel, out_shape=shapes, in_specs=[VMEM] * len(args), out_specs=specs, compiler_params=params()
    )(*args)


def dot(left, right, contract=((1,), (0,))):
    return lax.dot_general(left, right, (contract, ((), ())), preferred_element_type=F32)


def lookup(indices, table):
    chosen = indices[:, None] == jnp.arange(table.shape[0], dtype=jnp.int32)[None, :]
    return jnp.sum(jnp.where(chosen, table[None, :], jnp.zeros((), table.dtype)), axis=1)


def pack_columns(amp_ref, label_cd_ref, label_ij_ref, slot_ref, out_ref):
    keep = label_cd_ref[...] == label_ij_ref[...]
    masked = jnp.where(keep, amp_ref[...].astype(F32), 0.0).astype(BF16)
    rows = lax.broadcasted_iota(jnp.int32, (SLOTS, PAIRS), 0)
    place = jnp.where(rows == slot_ref[...], 1.0, 0.0).astype(BF16)
    out_ref[0] = dot(masked, place, ((1,), (1,))).astype(BF16)


def turn_rows(rows_ref, out_ref):
    row = lax.broadcasted_iota(jnp.int32, (ROWS, LANES), 0)
    lane = lax.broadcasted_iota(jnp.int32, (ROWS, LANES), 1)
    low = dot(rows_ref[...], jnp.where(lane == row, 1.0, 0.0).astype(BF16), ((0,), (0,)))
    high = dot(rows_ref[...], jnp.where(lane == row + 64, 1.0, 0.0).astype(BF16), ((0,), (0,)))
    half = CDS // 2
    for dest in range(CD // CDS):
        at = dest * CDS
        out_ref[dest] = (low[at : at + half] + high[at + half : at + CDS]).astype(BF16)


def by_partner(got_ref, out_ref):
    half = CDS // 2
    lane = lax.broadcasted_iota(jnp.int32, (half, LANES), 1)
    inside = [(lane >= OWN * a) & (lane < OWN * (a + 1)) for a in range(OWN)]
    for partner in range(16):
        halves = []
        for h in range(2):
            block = jnp.zeros((half, LANES), F32)
            for a in range(OWN):
                granule = a * 16 + partner
                source, piece = granule // 5, granule % 5
                shift = (OWN * a - 64 * h - OWN * piece) % LANES
                moved = got_ref[source].astype(F32)
                if shift:
                    moved = pltpu.roll(moved, shift, axis=1)
                block = jnp.where(inside[a], moved, block)
            halves.append(block)
        out_ref[partner] = jnp.concatenate(halves, axis=0).astype(BF16)


def difference(own_ref, mirror_ref, swap_ref, label_ab_ref, label_cd_ref, out_ref):
    label_cd = label_cd_ref[...]
    lane = lax.broadcasted_iota(jnp.int32, (CDS, LANES), 1)
    blocks = [jnp.zeros((CDS, LANES), F32) for _ in range(4)]
    for slab in range(2):
        for odd in range(2):
            packed = jnp.zeros((CDS, LANES), F32)
            for quarter in range(4):
                partner = 8 * slab + 2 * quarter + odd
                mirrored = dot(mirror_ref[partner], swap_ref[...])
                diff = own_ref[partner].astype(F32) - mirrored
                keep = label_ab_ref[partner : partner + 1, :] == label_cd
                packed = jnp.where(keep, diff, packed)
            first = 100 * (2 * slab + odd)
            if first:
                packed = pltpu.roll(packed, first % LANES, axis=1)
            for index in range(4):
                low, high = max(first - LANES * index, 0), min(first + 100 - LANES * index, LANES)
                if low < high:
                    blocks[index] = jnp.where((lane >= low) & (lane < high), packed, blocks[index])
    rest = blocks[3][0:8]
    for group in range(1, 6):
        rest = rest + pltpu.roll(blocks[3][8 * group : 8 * group + 8], 16 * group, axis=1)
    whole = jnp.concatenate([*blocks[:3], rest], axis=0).astype(BF16)
    for copy in range(32):
        out_ref[copy] = whole


def turn_back(got_ref, place_ref, rest_ref, out_ref):
    for source in range(32):
        piece = got_ref[source, 144:152, :].astype(F32)
        groups = [piece] + [pltpu.roll(piece, LANES - 16 * group, axis=1) for group in range(1, 6)]
        rest_ref[CDS * source : CDS * source + CDS, :] = jnp.concatenate(groups, axis=0).astype(BF16)
    for part in range(4):
        at = 384 * part
        total = dot(place_ref[3], rest_ref[at : at + 384, :], ((1,), (1,)))
        for index in range(3):
            block = got_ref[8 * part : 8 * part + 8, CDS * index : CDS * index + CDS, :].reshape(384, LANES)
            total = total + dot(place_ref[index], block, ((1,), (1,)))
        out_ref[:, at : at + 384] = total.astype(BF16)


def finish(got_ref, turn_ref, six_ref, core_six_ref, last_ref, core_last_ref, pick_ref, vir_ref, own_label_ref, own_energy_ref, label_b_ref,
           spread_label_b_ref, energy_b_ref, label_cd_ref, label_ij_ref, energy_ij_ref, slot_ref, out_ref,
           rest_ref, rows_ref, amp_ref, place_ref, left_ref):
    step = pl.program_id(0)

    @pl.when(step == 0)
    def _():
        turn_back(got_ref, turn_ref, rest_ref, rows_ref)
        rows = lax.broadcasted_iota(jnp.int32, (SLOTS, PAIRS), 0)
        place_ref[...] = jnp.where(rows == slot_ref[...], 1.0, 0.0).astype(BF16)
        six, last = (0, 1, 2, 3, 6, 7), (4, 5)
        for part, core, chips in ((six_ref, 0, six), (core_six_ref, 1, six), (last_ref, 0, last), (core_last_ref, 1, last)):
            for index, chip in enumerate(chips):
                source = ((vir_ref[0] ^ core) + 2 * chip) & 15
                amp_ref[pl.ds(pl.multiple_of(96 * source, 96), 96), :] = part[index]

    for a in range(STEP):
        label_a = own_label_ref[step * STEP + a]
        for part in range(4):
            wanted = label_cd_ref[:, 384 * part : 384 * part + 384] ^ label_a
            own = pl.ds(pl.multiple_of(48 * (step * STEP + a), 48), 48)
            values = rows_ref[own, 384 * part : 384 * part + 384].astype(F32)
            for quarter in range(4):
                keep = spread_label_b_ref[48 * quarter : 48 * quarter + 48, :] == wanted
                at = 192 * a + 48 * quarter
                left_ref[at : at + 48, 384 * part : 384 * part + 384] = jnp.where(keep, values, 0.0).astype(BF16)
    total = dot(left_ref[...], amp_ref[...]).astype(BF16)
    picked = [dot(pick_ref[...], total[192 * a : 192 * a + 192]).astype(BF16) for a in range(STEP)]
    ladder = dot(jnp.concatenate(picked, axis=0), place_ref[...])
    for a in range(STEP):
        label_a = own_label_ref[step * STEP + a]
        energy_a = own_energy_ref[step * STEP + a]
        update = ladder[NW * a : NW * a + NW] / ((energy_ij_ref[...] - energy_a) - energy_b_ref[...])
        keep = label_b_ref[...] == (label_ij_ref[...] ^ label_a)
        out_ref[NW * a : NW * a + NW, :] = jnp.where(keep, update, 0.0).astype(BF16)


def swap_table():
    table = np.zeros((LANES, LANES), np.float32)
    for a in range(OWN):
        for b in range(OWN):
            table[b * OWN + a, a * OWN + b] = 1.0
    return table


def place_table():
    table = np.zeros((4, 480, LANES), np.float32)
    for a in range(OWN):
        for part in range(4):
            for b in range(OWN):
                column = 100 * part + OWN * a + b
                table[column // LANES, 48 * a + OWN * part + b, column % LANES] = 1.0
    return table


def pick_table():
    table = np.zeros((NW, 192), np.float32)
    for b in range(NW):
        slab, within = b // SLAB, b % SLAB
        table[b, 48 * (within // 20) + 20 * slab + within % 20] = 1.0
    return table


def on_device(pair_integrals, amplitudes, vir_irrep, occ_irrep, pair_irrep, vir_energy, occ_energy):
    occ = lax.axis_index("occ")
    vir = lax.axis_index("vir")

    labels_vir = vir_irrep.reshape(-1)
    own_labels = lax.dynamic_slice_in_dim(labels_vir, vir * OWN, OWN)
    own_energy = lax.dynamic_slice_in_dim(vir_energy, vir * OWN, OWN)
    label_ab = jnp.bitwise_xor(own_labels[:, None], labels_vir[None, :])
    occ_pair = occ * PAIRS + jnp.arange(PAIRS, dtype=jnp.int32)
    first_occ = occ_pair // NOCC
    second_occ = occ_pair % NOCC
    label_ij = jnp.bitwise_xor(lookup(first_occ, occ_irrep), lookup(second_occ, occ_irrep))[None, :]
    energy_ij = (lookup(first_occ, occ_energy) + lookup(second_occ, occ_energy))[None, :]
    slot = ((first_occ - (occ * PAIRS) // NOCC) * 50 + second_occ % 50)[None, :]

    label_rows = lax.dynamic_slice_in_dim(pair_irrep, vir * 96, 96)[:, None]
    packed_amp = call(
        pack_columns, jax.ShapeDtypeStruct((1, 96, SLOTS), BF16), (amplitudes, label_rows, label_ij, slot)
    )

    from_chip = lambda array, k: lax.ppermute(array, "vir", [(i, (i - 2 * k) % 16) for i in range(16)])

    turned = call(turn_rows, jax.ShapeDtypeStruct((32, CDS // 2, LANES), BF16), (pair_integrals,))
    slices = lax.all_to_all(turned, "occ", split_axis=0, concat_axis=0, tiled=True)
    blocks = call(by_partner, jax.ShapeDtypeStruct((16, CDS, LANES), BF16), (slices,))
    blocks, packed_amp = lax.optimization_barrier((blocks, packed_amp))
    amp_pair = jnp.concatenate([packed_amp, from_chip(packed_amp, 1)], axis=0)
    mirror = lax.all_to_all(blocks, "vir", split_axis=0, concat_axis=0, tiled=True)
    block_labels = label_ab.reshape(OWN, 16, OWN).transpose(1, 0, 2).reshape(16, OWN * OWN)
    block_labels = jnp.pad(block_labels, ((0, 0), (0, LANES - OWN * OWN)), constant_values=-1)
    label_cds = lax.dynamic_slice_in_dim(pair_irrep, occ * CDS, CDS)[:, None]
    copies = call(
        difference,
        jax.ShapeDtypeStruct((32, 152, LANES), BF16),
        (blocks, mirror, jnp.asarray(swap_table(), BF16), block_labels, label_cds),
    )
    copies, amp_pair = lax.optimization_barrier((copies, amp_pair))
    amp_above = from_chip(amp_pair, 2)
    amp_six = jnp.concatenate([amp_pair, amp_above, from_chip(amp_pair, 6)], axis=0)
    from_core = lambda array: lax.ppermute(array, "vir", [(i, i ^ 1) for i in range(16)])
    amp_last, core_six = lax.optimization_barrier((from_chip(amp_above, 2), from_core(amp_six)))
    amp_parts = (amp_six, core_six, amp_last, from_core(amp_last))
    gathered = lax.all_to_all(copies, "occ", split_axis=0, concat_axis=0, tiled=True)

    spread_labels = jnp.pad(
        labels_vir.reshape(2, 4, 20).transpose(1, 0, 2).reshape(4, 40), ((0, 0), (0, 8)), constant_values=-1
    ).reshape(192, 1)
    whole = lambda *shape: pl.BlockSpec(shape, lambda i: (0,) * len(shape))
    scalars = pl.BlockSpec(memory_space=pltpu.SMEM)
    return pl.pallas_call(
        finish,
        grid=(OWN // STEP,),
        out_shape=jax.ShapeDtypeStruct((OWN * NW, PAIRS), BF16),
        in_specs=[
            whole(32, 152, LANES),
            whole(4, 480, LANES),
            whole(6, 96, SLOTS),
            whole(6, 96, SLOTS),
            whole(2, 96, SLOTS),
            whole(2, 96, SLOTS),
            whole(NW, 192),
            scalars,
            scalars,
            scalars,
            whole(NW, 1),
            whole(192, 1),
            whole(NW, 1),
            whole(1, CD),
            whole(1, PAIRS),
            whole(1, PAIRS),
            whole(1, PAIRS),
        ],
        out_specs=pl.BlockSpec((STEP * NW, PAIRS), lambda i: (i, 0)),
        scratch_shapes=[
            pltpu.VMEM((CD, LANES), BF16),
            pltpu.VMEM((480, CD), BF16),
            pltpu.VMEM((CD, SLOTS), BF16),
            pltpu.VMEM((SLOTS, PAIRS), BF16),
            pltpu.VMEM((STEP * 192, CD), BF16),
        ],
        compiler_params=params(),
    )(
        gathered,
        jnp.asarray(place_table(), BF16),
        *amp_parts,
        jnp.asarray(pick_table(), BF16),
        vir.reshape(1),
        own_labels,
        own_energy,
        labels_vir[:, None],
        spread_labels,
        vir_energy[:, None],
        pair_irrep[None, :],
        label_ij,
        energy_ij,
        slot,
    )


def solution(mesh):
    in_specs = (P(("vir", "occ"), None), P("vir", "occ"), P(), P(), P(), P(), P())
    out_specs = P("vir", "occ")
    return jax.shard_map(
        on_device, mesh=mesh, in_specs=in_specs, out_specs=out_specs, check_vma=False
    )
```

```python
import jax
import jax.numpy as jnp
import numpy as np
from jax import lax
from jax.experimental import pallas as pl
from jax.experimental.pallas import tpu as pltpu
from jax.sharding import PartitionSpec as P

SLAB = 80
NW = 160
NOCC = 200
CD = 1536
PAIRS = 1250
OWN = 10
ROWS = 50
CDS = 48
SLOTS = 384
LANES = 128
STEP = 2
F32 = jnp.float32
BF16 = jnp.bfloat16
VMEM = pl.BlockSpec(memory_space=pltpu.VMEM)


def params():
    return pltpu.CompilerParams(vmem_limit_bytes=48 * 1024 * 1024)


def call(kernel, shapes, args):
    specs = jax.tree.map(lambda _: VMEM, shapes)
    return pl.pallas_call(
        kernel, out_shape=shapes, in_specs=[VMEM] * len(args), out_specs=specs, compiler_params=params()
    )(*args)


def dot(left, right, contract=((1,), (0,))):
    return lax.dot_general(left, right, (contract, ((), ())), preferred_element_type=F32)


def lookup(indices, table):
    chosen = indices[:, None] == jnp.arange(table.shape[0], dtype=jnp.int32)[None, :]
    return jnp.sum(jnp.where(chosen, table[None, :], jnp.zeros((), table.dtype)), axis=1)


def pack_columns(amp_ref, label_cd_ref, label_ij_ref, slot_ref, out_ref, place_ref):
    keep = label_cd_ref[...] == label_ij_ref[...]
    masked = jnp.where(keep, amp_ref[...].astype(F32), 0.0).astype(BF16)
    rows = lax.broadcasted_iota(jnp.int32, (SLOTS, PAIRS), 0)
    place = jnp.where(rows == slot_ref[...], 1.0, 0.0).astype(BF16)
    place_ref[...] = place
    out_ref[0] = dot(masked, place, ((1,), (1,))).astype(BF16)


def turn_rows(rows_ref, out_ref):
    row = lax.broadcasted_iota(jnp.int32, (ROWS, LANES), 0)
    lane = lax.broadcasted_iota(jnp.int32, (ROWS, LANES), 1)
    low = dot(rows_ref[...], jnp.where(lane == row, 1.0, 0.0).astype(BF16), ((0,), (0,)))
    high = dot(rows_ref[...], jnp.where(lane == row + 64, 1.0, 0.0).astype(BF16), ((0,), (0,)))
    half = CDS // 2
    for dest in range(CD // CDS):
        at = dest * CDS
        out_ref[dest] = (low[at : at + half] + high[at + half : at + CDS]).astype(BF16)


def by_partner(got_ref, out_ref):
    half = CDS // 2
    lane = lax.broadcasted_iota(jnp.int32, (half, LANES), 1)
    inside = [(lane >= OWN * a) & (lane < OWN * (a + 1)) for a in range(OWN)]
    for partner in range(16):
        halves = []
        for h in range(2):
            block = jnp.zeros((half, LANES), F32)
            for a in range(OWN):
                granule = a * 16 + partner
                source, piece = granule // 5, granule % 5
                shift = (OWN * a - 64 * h - OWN * piece) % LANES
                moved = got_ref[source].astype(F32)
                if shift:
                    moved = pltpu.roll(moved, shift, axis=1)
                block = jnp.where(inside[a], moved, block)
            halves.append(block)
        out_ref[partner] = jnp.concatenate(halves, axis=0).astype(BF16)


def difference(own_ref, mirror_ref, swap_ref, label_ab_ref, label_cd_ref, out_ref):
    label_cd = label_cd_ref[...]
    lane = lax.broadcasted_iota(jnp.int32, (CDS, LANES), 1)
    blocks = [jnp.zeros((CDS, LANES), F32) for _ in range(4)]
    mirrored = dot(mirror_ref[...].reshape(16 * CDS, LANES), swap_ref[...])
    for slab in range(2):
        for odd in range(2):
            packed = jnp.zeros((CDS, LANES), F32)
            for quarter in range(4):
                partner = 8 * slab + 2 * quarter + odd
                diff = own_ref[partner].astype(F32) - mirrored[CDS * partner : CDS * partner + CDS]
                keep = label_ab_ref[partner : partner + 1, :] == label_cd
                packed = jnp.where(keep, diff, packed)
            first = 100 * (2 * slab + odd)
            if first:
                packed = pltpu.roll(packed, first % LANES, axis=1)
            for index in range(4):
                low, high = max(first - LANES * index, 0), min(first + 100 - LANES * index, LANES)
                if low < high:
                    blocks[index] = jnp.where((lane >= low) & (lane < high), packed, blocks[index])
    rest = blocks[3][0:8]
    for group in range(1, 6):
        rest = rest + pltpu.roll(blocks[3][8 * group : 8 * group + 8], 16 * group, axis=1)
    whole = jnp.concatenate([*blocks[:3], rest], axis=0).astype(BF16)
    for copy in range(32):
        out_ref[copy] = whole


def turn_back(got_ref, place_ref, rest_ref, out_ref):
    for source in range(32):
        piece = got_ref[source, 144:152, :].astype(F32)
        groups = [piece] + [pltpu.roll(piece, LANES - 16 * group, axis=1) for group in range(1, 6)]
        rest_ref[CDS * source : CDS * source + CDS, :] = jnp.concatenate(groups, axis=0).astype(BF16)
    for part in range(4):
        at = 384 * part
        total = dot(place_ref[3], rest_ref[at : at + 384, :], ((1,), (1,)))
        for index in range(3):
            block = got_ref[8 * part : 8 * part + 8, CDS * index : CDS * index + CDS, :].reshape(384, LANES)
            total = total + dot(place_ref[index], block, ((1,), (1,)))
        out_ref[:, at : at + 384] = total.astype(BF16)


def finish(got_ref, turn_ref, six_ref, core_six_ref, last_ref, core_last_ref, place_ref, pick_ref, vir_ref,
           own_label_ref, own_energy_ref, label_b_ref, spread_label_b_ref, energy_b_ref, label_cd_ref, label_ij_ref,
           energy_ij_ref, out_ref, rest_ref, rows_ref, amp_ref, left_ref, picked_ref):
    step = pl.program_id(0)

    @pl.when(step == 0)
    def _():
        six, last = (0, 1, 2, 3, 6, 7), (4, 5)
        for part, core, chips in ((six_ref, 0, six), (core_six_ref, 1, six), (last_ref, 0, last), (core_last_ref, 1, last)):
            for index, chip in enumerate(chips):
                source = ((vir_ref[0] ^ core) + 2 * chip) & 15
                amp_ref[pl.ds(pl.multiple_of(96 * source, 96), 96), :] = part[index]
        turn_back(got_ref, turn_ref, rest_ref, rows_ref)
        for a in range(OWN):
            label_a = own_label_ref[a]
            for part in range(4):
                lanes = slice(384 * part, 384 * part + 384)
                wanted = label_cd_ref[:, lanes] ^ label_a
                values = rows_ref[48 * a : 48 * a + 48, lanes].astype(F32)
                for quarter in range(4):
                    keep = spread_label_b_ref[48 * quarter : 48 * quarter + 48, :] == wanted
                    at = 192 * a + 48 * quarter
                    left_ref[at : at + 48, lanes] = jnp.where(keep, values, 0.0).astype(BF16)
        total = dot(left_ref[...], amp_ref[...]).astype(BF16)
        for a in range(OWN):
            rows = dot(pick_ref[...], total[192 * a : 192 * a + 192]).astype(BF16)
            picked_ref[NW * a : NW * a + NW, :] = rows

    own = pl.ds(pl.multiple_of(STEP * NW * step, STEP * NW), STEP * NW)
    ladder = dot(picked_ref[own, :], place_ref[...])
    for a in range(STEP):
        label_a = own_label_ref[step * STEP + a]
        energy_a = own_energy_ref[step * STEP + a]
        update = ladder[NW * a : NW * a + NW] / ((energy_ij_ref[...] - energy_a) - energy_b_ref[...])
        keep = label_b_ref[...] == (label_ij_ref[...] ^ label_a)
        out_ref[NW * a : NW * a + NW, :] = jnp.where(keep, update, 0.0).astype(BF16)


def swap_table():
    table = np.zeros((LANES, LANES), np.float32)
    for a in range(OWN):
        for b in range(OWN):
            table[b * OWN + a, a * OWN + b] = 1.0
    return table


def place_table():
    table = np.zeros((4, 480, LANES), np.float32)
    for a in range(OWN):
        for part in range(4):
            for b in range(OWN):
                column = 100 * part + OWN * a + b
                table[column // LANES, 48 * a + OWN * part + b, column % LANES] = 1.0
    return table


def pick_table():
    table = np.zeros((NW, 192), np.float32)
    for b in range(NW):
        slab, within = b // SLAB, b % SLAB
        table[b, 48 * (within // 20) + 20 * slab + within % 20] = 1.0
    return table


def on_device(pair_integrals, amplitudes, vir_irrep, occ_irrep, pair_irrep, vir_energy, occ_energy):
    occ = lax.axis_index("occ")
    vir = lax.axis_index("vir")

    labels_vir = vir_irrep.reshape(-1)
    own_labels = lax.dynamic_slice_in_dim(labels_vir, vir * OWN, OWN)
    own_energy = lax.dynamic_slice_in_dim(vir_energy, vir * OWN, OWN)
    label_ab = jnp.bitwise_xor(own_labels[:, None], labels_vir[None, :])
    occ_pair = occ * PAIRS + jnp.arange(PAIRS, dtype=jnp.int32)
    first_occ = occ_pair // NOCC
    second_occ = occ_pair % NOCC
    label_ij = jnp.bitwise_xor(lookup(first_occ, occ_irrep), lookup(second_occ, occ_irrep))[None, :]
    energy_ij = (lookup(first_occ, occ_energy) + lookup(second_occ, occ_energy))[None, :]
    slot = ((first_occ - (occ * PAIRS) // NOCC) * 50 + second_occ % 50)[None, :]

    label_rows = lax.dynamic_slice_in_dim(pair_irrep, vir * 96, 96)[:, None]
    packed_amp, place_columns = call(
        pack_columns,
        (jax.ShapeDtypeStruct((1, 96, SLOTS), BF16), jax.ShapeDtypeStruct((SLOTS, PAIRS), BF16)),
        (amplitudes, label_rows, label_ij, slot),
    )

    from_chip = lambda array, k: lax.ppermute(array, "vir", [(i, (i - 2 * k) % 16) for i in range(16)])

    turned = call(turn_rows, jax.ShapeDtypeStruct((32, CDS // 2, LANES), BF16), (pair_integrals,))
    slices = lax.all_to_all(turned, "occ", split_axis=0, concat_axis=0, tiled=True)
    blocks = call(by_partner, jax.ShapeDtypeStruct((16, CDS, LANES), BF16), (slices,))
    blocks, packed_amp = lax.optimization_barrier((blocks, packed_amp))
    amp_pair = jnp.concatenate([packed_amp, from_chip(packed_amp, 1)], axis=0)
    mirror = lax.all_to_all(blocks, "vir", split_axis=0, concat_axis=0, tiled=True)
    block_labels = label_ab.reshape(OWN, 16, OWN).transpose(1, 0, 2).reshape(16, OWN * OWN)
    block_labels = jnp.pad(block_labels, ((0, 0), (0, LANES - OWN * OWN)), constant_values=-1)
    label_cds = lax.dynamic_slice_in_dim(pair_irrep, occ * CDS, CDS)[:, None]
    copies = call(
        difference,
        jax.ShapeDtypeStruct((32, 152, LANES), BF16),
        (blocks, mirror, jnp.asarray(swap_table(), BF16), block_labels, label_cds),
    )
    copies, amp_pair = lax.optimization_barrier((copies, amp_pair))
    amp_above = from_chip(amp_pair, 2)
    amp_six = jnp.concatenate([amp_pair, amp_above, from_chip(amp_pair, 6)], axis=0)
    from_core = lambda array: lax.ppermute(array, "vir", [(i, i ^ 1) for i in range(16)])
    amp_last, core_six = lax.optimization_barrier((from_chip(amp_above, 2), from_core(amp_six)))
    amp_parts = (amp_six, core_six, amp_last, from_core(amp_last))
    gathered = lax.all_to_all(copies, "occ", split_axis=0, concat_axis=0, tiled=True)

    spread_labels = jnp.pad(
        labels_vir.reshape(2, 4, 20).transpose(1, 0, 2).reshape(4, 40), ((0, 0), (0, 8)), constant_values=-1
    ).reshape(192, 1)
    whole = lambda *shape: pl.BlockSpec(shape, lambda i: (0,) * len(shape))
    scalars = pl.BlockSpec(memory_space=pltpu.SMEM)
    return pl.pallas_call(
        finish,
        grid=(OWN // STEP,),
        out_shape=jax.ShapeDtypeStruct((OWN * NW, PAIRS), BF16),
        in_specs=[
            whole(32, 152, LANES),
            whole(4, 480, LANES),
            whole(6, 96, SLOTS),
            whole(6, 96, SLOTS),
            whole(2, 96, SLOTS),
            whole(2, 96, SLOTS),
            whole(SLOTS, PAIRS),
            whole(NW, 192),
            scalars,
            scalars,
            scalars,
            whole(NW, 1),
            whole(192, 1),
            whole(NW, 1),
            whole(1, CD),
            whole(1, PAIRS),
            whole(1, PAIRS),
        ],
        out_specs=pl.BlockSpec((STEP * NW, PAIRS), lambda i: (i, 0)),
        scratch_shapes=[
            pltpu.VMEM((CD, LANES), BF16),
            pltpu.VMEM((480, CD), BF16),
            pltpu.VMEM((CD, SLOTS), BF16),
            pltpu.VMEM((OWN * 192, CD), BF16),
            pltpu.VMEM((OWN * NW, SLOTS), BF16),
        ],
        compiler_params=params(),
    )(
        gathered,
        jnp.asarray(place_table(), BF16),
        *amp_parts,
        place_columns,
        jnp.asarray(pick_table(), BF16),
        vir.reshape(1),
        own_labels,
        own_energy,
        labels_vir[:, None],
        spread_labels,
        vir_energy[:, None],
        pair_irrep[None, :],
        label_ij,
        energy_ij,
    )


def solution(mesh):
    in_specs = (P(("vir", "occ"), None), P("vir", "occ"), P(), P(), P(), P(), P())
    out_specs = P("vir", "occ")
    return jax.shard_map(
        on_device, mesh=mesh, in_specs=in_specs, out_specs=out_specs, check_vma=False
    )
```

```python
import jax
import jax.numpy as jnp
import numpy as np
from jax import lax
from jax.experimental import pallas as pl
from jax.experimental.pallas import tpu as pltpu
from jax.sharding import PartitionSpec as P

SLAB = 80
NW = 160
NOCC = 200
CD = 1536
PAIRS = 1250
OWN = 10
ROWS = 50
CDS = 48
SLOTS = 384
LANES = 128
STEP = 5
F32 = jnp.float32
BF16 = jnp.bfloat16
VMEM = pl.BlockSpec(memory_space=pltpu.VMEM)


def params():
    return pltpu.CompilerParams(vmem_limit_bytes=48 * 1024 * 1024)


def call(kernel, shapes, args):
    specs = jax.tree.map(lambda _: VMEM, shapes)
    return pl.pallas_call(
        kernel, out_shape=shapes, in_specs=[VMEM] * len(args), out_specs=specs, compiler_params=params()
    )(*args)


def dot(left, right, contract=((1,), (0,))):
    return lax.dot_general(left, right, (contract, ((), ())), preferred_element_type=F32)


def lookup(indices, table):
    chosen = indices[:, None] == jnp.arange(table.shape[0], dtype=jnp.int32)[None, :]
    return jnp.sum(jnp.where(chosen, table[None, :], jnp.zeros((), table.dtype)), axis=1)


def pack_columns(amp_ref, label_cd_ref, label_ij_ref, slot_ref, out_ref, place_ref):
    keep = label_cd_ref[...] == label_ij_ref[...]
    masked = jnp.where(keep, amp_ref[...].astype(F32), 0.0).astype(BF16)
    rows = lax.broadcasted_iota(jnp.int32, (SLOTS, PAIRS), 0)
    place = jnp.where(rows == slot_ref[...], 1.0, 0.0).astype(BF16)
    place_ref[...] = place
    out_ref[0] = dot(masked, place, ((1,), (1,))).astype(BF16)


def turn_rows(rows_ref, out_ref):
    row = lax.broadcasted_iota(jnp.int32, (ROWS, LANES), 0)
    lane = lax.broadcasted_iota(jnp.int32, (ROWS, LANES), 1)
    low = dot(rows_ref[...], jnp.where(lane == row, 1.0, 0.0).astype(BF16), ((0,), (0,)))
    high = dot(rows_ref[...], jnp.where(lane == row + 64, 1.0, 0.0).astype(BF16), ((0,), (0,)))
    half = CDS // 2
    for dest in range(CD // CDS):
        at = dest * CDS
        out_ref[dest] = (low[at : at + half] + high[at + half : at + CDS]).astype(BF16)


def by_partner(got_ref, out_ref):
    half = CDS // 2
    lane = lax.broadcasted_iota(jnp.int32, (half, LANES), 1)
    inside = [(lane >= OWN * a) & (lane < OWN * (a + 1)) for a in range(OWN)]
    for partner in range(16):
        halves = []
        for h in range(2):
            block = jnp.zeros((half, LANES), F32)
            for a in range(OWN):
                granule = a * 16 + partner
                source, piece = granule // 5, granule % 5
                shift = (OWN * a - 64 * h - OWN * piece) % LANES
                moved = got_ref[source].astype(F32)
                if shift:
                    moved = pltpu.roll(moved, shift, axis=1)
                block = jnp.where(inside[a], moved, block)
            halves.append(block)
        out_ref[partner] = jnp.concatenate(halves, axis=0).astype(BF16)


def difference(own_ref, mirror_ref, swap_ref, label_ab_ref, label_cd_ref, out_ref):
    label_cd = label_cd_ref[...]
    lane = lax.broadcasted_iota(jnp.int32, (CDS, LANES), 1)
    blocks = [jnp.zeros((CDS, LANES), F32) for _ in range(4)]
    mirrored = dot(mirror_ref[...].reshape(16 * CDS, LANES), swap_ref[...])
    for slab in range(2):
        for odd in range(2):
            packed = jnp.zeros((CDS, LANES), F32)
            for quarter in range(4):
                partner = 8 * slab + 2 * quarter + odd
                diff = own_ref[partner].astype(F32) - mirrored[CDS * partner : CDS * partner + CDS]
                keep = label_ab_ref[partner : partner + 1, :] == label_cd
                packed = jnp.where(keep, diff, packed)
            first = 100 * (2 * slab + odd)
            if first:
                packed = pltpu.roll(packed, first % LANES, axis=1)
            for index in range(4):
                low, high = max(first - LANES * index, 0), min(first + 100 - LANES * index, LANES)
                if low < high:
                    blocks[index] = jnp.where((lane >= low) & (lane < high), packed, blocks[index])
    rest = blocks[3][0:8]
    for group in range(1, 6):
        rest = rest + pltpu.roll(blocks[3][8 * group : 8 * group + 8], 16 * group, axis=1)
    whole = jnp.concatenate([*blocks[:3], rest], axis=0).astype(BF16)
    for copy in range(32):
        out_ref[copy] = whole


def turn_back(got_ref, place_ref, rest_ref, out_ref):
    for source in range(32):
        piece = got_ref[source, 144:152, :].astype(F32)
        groups = [piece] + [pltpu.roll(piece, LANES - 16 * group, axis=1) for group in range(1, 6)]
        rest_ref[CDS * source : CDS * source + CDS, :] = jnp.concatenate(groups, axis=0).astype(BF16)
    for part in range(4):
        at = 384 * part
        total = dot(place_ref[3], rest_ref[at : at + 384, :], ((1,), (1,)))
        for index in range(3):
            block = got_ref[8 * part : 8 * part + 8, CDS * index : CDS * index + CDS, :].reshape(384, LANES)
            total = total + dot(place_ref[index], block, ((1,), (1,)))
        out_ref[:, at : at + 384] = total.astype(BF16)


def finish(got_ref, turn_ref, pair_ref, core_pair_ref, most_ref, core_most_ref, place_ref, pick_ref, vir_ref, own_label_ref, own_energy_ref, label_b_ref,
           spread_label_b_ref, energy_b_ref, label_cd_ref, label_ij_ref, energy_ij_ref, out_ref,
           rest_ref, rows_ref, amp_ref, left_ref):
    step = pl.program_id(0)

    @pl.when(step == 0)
    def _():
        turn_back(got_ref, turn_ref, rest_ref, rows_ref)
        pair, most = (0, 1), (2, 3, 6, 7, 4, 5)
        for part, core, chips in ((pair_ref, 0, pair), (core_pair_ref, 1, pair), (most_ref, 0, most), (core_most_ref, 1, most)):
            for index, chip in enumerate(chips):
                source = ((vir_ref[0] ^ core) + 2 * chip) & 15
                amp_ref[pl.ds(pl.multiple_of(96 * source, 96), 96), :] = part[index]

    for a in range(STEP):
        label_a = own_label_ref[step * STEP + a]
        for part in range(4):
            wanted = label_cd_ref[:, 384 * part : 384 * part + 384] ^ label_a
            own = pl.ds(pl.multiple_of(48 * (step * STEP + a), 48), 48)
            values = rows_ref[own, 384 * part : 384 * part + 384].astype(F32)
            for quarter in range(4):
                keep = spread_label_b_ref[48 * quarter : 48 * quarter + 48, :] == wanted
                at = 192 * a + 48 * quarter
                left_ref[at : at + 48, 384 * part : 384 * part + 384] = jnp.where(keep, values, 0.0).astype(BF16)
    total = dot(left_ref[...], amp_ref[...]).astype(BF16)
    picked = [dot(pick_ref[...], total[192 * a : 192 * a + 192]).astype(BF16) for a in range(STEP)]
    ladder = dot(jnp.concatenate(picked, axis=0), place_ref[...])
    for a in range(STEP):
        label_a = own_label_ref[step * STEP + a]
        energy_a = own_energy_ref[step * STEP + a]
        update = ladder[NW * a : NW * a + NW] / ((energy_ij_ref[...] - energy_a) - energy_b_ref[...])
        keep = label_b_ref[...] == (label_ij_ref[...] ^ label_a)
        out_ref[NW * a : NW * a + NW, :] = jnp.where(keep, update, 0.0).astype(BF16)


def swap_table():
    table = np.zeros((LANES, LANES), np.float32)
    for a in range(OWN):
        for b in range(OWN):
            table[b * OWN + a, a * OWN + b] = 1.0
    return table


def place_table():
    table = np.zeros((4, 480, LANES), np.float32)
    for a in range(OWN):
        for part in range(4):
            for b in range(OWN):
                column = 100 * part + OWN * a + b
                table[column // LANES, 48 * a + OWN * part + b, column % LANES] = 1.0
    return table


def pick_table():
    table = np.zeros((NW, 192), np.float32)
    for b in range(NW):
        slab, within = b // SLAB, b % SLAB
        table[b, 48 * (within // 20) + 20 * slab + within % 20] = 1.0
    return table


def on_device(pair_integrals, amplitudes, vir_irrep, occ_irrep, pair_irrep, vir_energy, occ_energy):
    occ = lax.axis_index("occ")
    vir = lax.axis_index("vir")

    labels_vir = vir_irrep.reshape(-1)
    own_labels = lax.dynamic_slice_in_dim(labels_vir, vir * OWN, OWN)
    own_energy = lax.dynamic_slice_in_dim(vir_energy, vir * OWN, OWN)
    label_ab = jnp.bitwise_xor(own_labels[:, None], labels_vir[None, :])
    occ_pair = occ * PAIRS + jnp.arange(PAIRS, dtype=jnp.int32)
    first_occ = occ_pair // NOCC
    second_occ = occ_pair % NOCC
    label_ij = jnp.bitwise_xor(lookup(first_occ, occ_irrep), lookup(second_occ, occ_irrep))[None, :]
    energy_ij = (lookup(first_occ, occ_energy) + lookup(second_occ, occ_energy))[None, :]
    slot = ((first_occ - (occ * PAIRS) // NOCC) * 50 + second_occ % 50)[None, :]

    label_rows = lax.dynamic_slice_in_dim(pair_irrep, vir * 96, 96)[:, None]
    packed_amp, place_columns = call(
        pack_columns,
        (jax.ShapeDtypeStruct((1, 96, SLOTS), BF16), jax.ShapeDtypeStruct((SLOTS, PAIRS), BF16)),
        (amplitudes, label_rows, label_ij, slot),
    )

    from_chip = lambda array, k: lax.ppermute(array, "vir", [(i, (i - 2 * k) % 16) for i in range(16)])

    turned = call(turn_rows, jax.ShapeDtypeStruct((32, CDS // 2, LANES), BF16), (pair_integrals,))
    slices = lax.all_to_all(turned, "occ", split_axis=0, concat_axis=0, tiled=True)
    blocks = call(by_partner, jax.ShapeDtypeStruct((16, CDS, LANES), BF16), (slices,))
    blocks, packed_amp = lax.optimization_barrier((blocks, packed_amp))
    amp_pair = jnp.concatenate([packed_amp, from_chip(packed_amp, 1)], axis=0)
    mirror = lax.all_to_all(blocks, "vir", split_axis=0, concat_axis=0, tiled=True)
    block_labels = label_ab.reshape(OWN, 16, OWN).transpose(1, 0, 2).reshape(16, OWN * OWN)
    block_labels = jnp.pad(block_labels, ((0, 0), (0, LANES - OWN * OWN)), constant_values=-1)
    label_cds = lax.dynamic_slice_in_dim(pair_irrep, occ * CDS, CDS)[:, None]
    copies = call(
        difference,
        jax.ShapeDtypeStruct((32, 152, LANES), BF16),
        (blocks, mirror, jnp.asarray(swap_table(), BF16), block_labels, label_cds),
    )
    copies, amp_pair = lax.optimization_barrier((copies, amp_pair))
    from_core = lambda array: lax.ppermute(array, "vir", [(i, i ^ 1) for i in range(16)])
    amp_above, amp_below, core_pair = lax.optimization_barrier(
        (from_chip(amp_pair, 2), from_chip(amp_pair, 6), from_core(amp_pair))
    )
    amp_rest = jnp.concatenate([amp_above, amp_below, from_chip(amp_above, 2)], axis=0)
    amp_parts = (amp_pair, core_pair, amp_rest, from_core(amp_rest))
    gathered = lax.all_to_all(copies, "occ", split_axis=0, concat_axis=0, tiled=True)

    spread_labels = jnp.pad(
        labels_vir.reshape(2, 4, 20).transpose(1, 0, 2).reshape(4, 40), ((0, 0), (0, 8)), constant_values=-1
    ).reshape(192, 1)
    whole = lambda *shape: pl.BlockSpec(shape, lambda i: (0,) * len(shape))
    scalars = pl.BlockSpec(memory_space=pltpu.SMEM)
    return pl.pallas_call(
        finish,
        grid=(OWN // STEP,),
        out_shape=jax.ShapeDtypeStruct((OWN * NW, PAIRS), BF16),
        in_specs=[
            whole(32, 152, LANES),
            whole(4, 480, LANES),
            whole(2, 96, SLOTS),
            whole(2, 96, SLOTS),
            whole(6, 96, SLOTS),
            whole(6, 96, SLOTS),
            whole(SLOTS, PAIRS),
            whole(NW, 192),
            scalars,
            scalars,
            scalars,
            whole(NW, 1),
            whole(192, 1),
            whole(NW, 1),
            whole(1, CD),
            whole(1, PAIRS),
            whole(1, PAIRS),
        ],
        out_specs=pl.BlockSpec((STEP * NW, PAIRS), lambda i: (i, 0)),
        scratch_shapes=[
            pltpu.VMEM((CD, LANES), BF16),
            pltpu.VMEM((480, CD), BF16),
            pltpu.VMEM((CD, SLOTS), BF16),
            pltpu.VMEM((STEP * 192, CD), BF16),
        ],
        compiler_params=params(),
    )(
        gathered,
        jnp.asarray(place_table(), BF16),
        *amp_parts,
        place_columns,
        jnp.asarray(pick_table(), BF16),
        vir.reshape(1),
        own_labels,
        own_energy,
        labels_vir[:, None],
        spread_labels,
        vir_energy[:, None],
        pair_irrep[None, :],
        label_ij,
        energy_ij,
    )


def solution(mesh):
    in_specs = (P(("vir", "occ"), None), P("vir", "occ"), P(), P(), P(), P(), P())
    out_specs = P("vir", "occ")
    return jax.shard_map(
        on_device, mesh=mesh, in_specs=in_specs, out_specs=out_specs, check_vma=False
    )
```

```python
import jax
import jax.numpy as jnp
import numpy as np
from jax import lax
from jax.experimental import pallas as pl
from jax.experimental.pallas import tpu as pltpu
from jax.sharding import PartitionSpec as P

SLAB = 80
NW = 160
NOCC = 200
CD = 1536
PAIRS = 1250
OWN = 10
ROWS = 50
CDS = 48
SLOTS = 384
LANES = 128
STEP = 5
F32 = jnp.float32
BF16 = jnp.bfloat16
VMEM = pl.BlockSpec(memory_space=pltpu.VMEM)


def params():
    return pltpu.CompilerParams(vmem_limit_bytes=48 * 1024 * 1024)


def call(kernel, shapes, args):
    specs = jax.tree.map(lambda _: VMEM, shapes)
    return pl.pallas_call(
        kernel, out_shape=shapes, in_specs=[VMEM] * len(args), out_specs=specs, compiler_params=params()
    )(*args)


def dot(left, right, contract=((1,), (0,))):
    return lax.dot_general(left, right, (contract, ((), ())), preferred_element_type=F32)


def lookup(indices, table):
    chosen = indices[:, None] == jnp.arange(table.shape[0], dtype=jnp.int32)[None, :]
    return jnp.sum(jnp.where(chosen, table[None, :], jnp.zeros((), table.dtype)), axis=1)


def pack_columns(amp_ref, label_cd_ref, label_ij_ref, slot_ref, out_ref):
    keep = label_cd_ref[...] == label_ij_ref[...]
    masked = jnp.where(keep, amp_ref[...].astype(F32), 0.0).astype(BF16)
    rows = lax.broadcasted_iota(jnp.int32, (SLOTS, PAIRS), 0)
    place = jnp.where(rows == slot_ref[...], 1.0, 0.0).astype(BF16)
    out_ref[0] = dot(masked, place, ((1,), (1,))).astype(BF16)


def turn_rows(rows_ref, out_ref):
    row = lax.broadcasted_iota(jnp.int32, (ROWS, LANES), 0)
    lane = lax.broadcasted_iota(jnp.int32, (ROWS, LANES), 1)
    low = dot(rows_ref[...], jnp.where(lane == row, 1.0, 0.0).astype(BF16), ((0,), (0,)))
    high = dot(rows_ref[...], jnp.where(lane == row + 64, 1.0, 0.0).astype(BF16), ((0,), (0,)))
    half = CDS // 2
    for dest in range(CD // CDS):
        at = dest * CDS
        out_ref[dest] = (low[at : at + half] + high[at + half : at + CDS]).astype(BF16)


def by_partner(got_ref, out_ref):
    half = CDS // 2
    lane = lax.broadcasted_iota(jnp.int32, (half, LANES), 1)
    inside = [(lane >= OWN * a) & (lane < OWN * (a + 1)) for a in range(OWN)]
    for partner in range(16):
        halves = []
        for h in range(2):
            block = jnp.zeros((half, LANES), F32)
            for a in range(OWN):
                granule = a * 16 + partner
                source, piece = granule // 5, granule % 5
                shift = (OWN * a - 64 * h - OWN * piece) % LANES
                moved = got_ref[source].astype(F32)
                if shift:
                    moved = pltpu.roll(moved, shift, axis=1)
                block = jnp.where(inside[a], moved, block)
            halves.append(block)
        out_ref[partner] = jnp.concatenate(halves, axis=0).astype(BF16)


def difference(own_ref, mirror_ref, swap_ref, label_ab_ref, label_cd_ref, out_ref):
    label_cd = label_cd_ref[...]
    lane = lax.broadcasted_iota(jnp.int32, (CDS, LANES), 1)
    blocks = [jnp.zeros((CDS, LANES), F32) for _ in range(4)]
    for slab in range(2):
        for odd in range(2):
            packed = jnp.zeros((CDS, LANES), F32)
            for quarter in range(4):
                partner = 8 * slab + 2 * quarter + odd
                mirrored = dot(mirror_ref[partner], swap_ref[...])
                diff = own_ref[partner].astype(F32) - mirrored
                keep = label_ab_ref[partner : partner + 1, :] == label_cd
                packed = jnp.where(keep, diff, packed)
            first = 100 * (2 * slab + odd)
            if first:
                packed = pltpu.roll(packed, first % LANES, axis=1)
            for index in range(4):
                low, high = max(first - LANES * index, 0), min(first + 100 - LANES * index, LANES)
                if low < high:
                    blocks[index] = jnp.where((lane >= low) & (lane < high), packed, blocks[index])
    rest = blocks[3][0:8]
    for group in range(1, 6):
        rest = rest + pltpu.roll(blocks[3][8 * group : 8 * group + 8], 16 * group, axis=1)
    whole = jnp.concatenate([*blocks[:3], rest], axis=0).astype(BF16)
    for copy in range(32):
        out_ref[copy] = whole


def turn_back(got_ref, place_ref, rest_ref, out_ref):
    for source in range(32):
        piece = got_ref[source, 144:152, :].astype(F32)
        groups = [piece] + [pltpu.roll(piece, LANES - 16 * group, axis=1) for group in range(1, 6)]
        rest_ref[CDS * source : CDS * source + CDS, :] = jnp.concatenate(groups, axis=0).astype(BF16)
    for part in range(4):
        at = 384 * part
        total = dot(place_ref[3], rest_ref[at : at + 384, :], ((1,), (1,)))
        for index in range(3):
            block = got_ref[8 * part : 8 * part + 8, CDS * index : CDS * index + CDS, :].reshape(384, LANES)
            total = total + dot(place_ref[index], block, ((1,), (1,)))
        out_ref[:, at : at + 384] = total.astype(BF16)


def finish(got_ref, turn_ref, six_ref, core_six_ref, last_ref, core_last_ref, pick_ref, vir_ref, own_label_ref, own_energy_ref, label_b_ref,
           spread_label_b_ref, energy_b_ref, label_cd_ref, label_ij_ref, energy_ij_ref, slot_ref, out_ref,
           rest_ref, rows_ref, amp_ref, place_ref, left_ref):
    step = pl.program_id(0)

    @pl.when(step == 0)
    def _():
        turn_back(got_ref, turn_ref, rest_ref, rows_ref)
        rows = lax.broadcasted_iota(jnp.int32, (SLOTS, PAIRS), 0)
        place_ref[...] = jnp.where(rows == slot_ref[...], 1.0, 0.0).astype(BF16)
        six, last = (0, 1, 2, 3, 6, 7), (4, 5)
        for part, core, chips in ((six_ref, 0, six), (core_six_ref, 1, six), (last_ref, 0, last), (core_last_ref, 1, last)):
            for index, chip in enumerate(chips):
                source = ((vir_ref[0] ^ core) + 2 * chip) & 15
                amp_ref[pl.ds(pl.multiple_of(96 * source, 96), 96), :] = part[index]

    total = jnp.zeros((STEP * 192, SLOTS), F32)
    for part in range(4):
        lanes = slice(384 * part, 384 * part + 384)
        for a in range(STEP):
            wanted = label_cd_ref[:, lanes] ^ own_label_ref[step * STEP + a]
            own = pl.ds(pl.multiple_of(48 * (step * STEP + a), 48), 48)
            values = rows_ref[own, lanes].astype(F32)
            for quarter in range(4):
                keep = spread_label_b_ref[48 * quarter : 48 * quarter + 48, :] == wanted
                at = 192 * a + 48 * quarter
                left_ref[part, at : at + 48, :] = jnp.where(keep, values, 0.0).astype(BF16)
        total = total + dot(left_ref[part], amp_ref[lanes, :])
    total = total.astype(BF16)
    picked = [dot(pick_ref[...], total[192 * a : 192 * a + 192]).astype(BF16) for a in range(STEP)]
    ladder = dot(jnp.concatenate(picked, axis=0), place_ref[...])
    for a in range(STEP):
        label_a = own_label_ref[step * STEP + a]
        energy_a = own_energy_ref[step * STEP + a]
        update = ladder[NW * a : NW * a + NW] / ((energy_ij_ref[...] - energy_a) - energy_b_ref[...])
        keep = label_b_ref[...] == (label_ij_ref[...] ^ label_a)
        out_ref[NW * a : NW * a + NW, :] = jnp.where(keep, update, 0.0).astype(BF16)


def swap_table():
    table = np.zeros((LANES, LANES), np.float32)
    for a in range(OWN):
        for b in range(OWN):
            table[b * OWN + a, a * OWN + b] = 1.0
    return table


def place_table():
    table = np.zeros((4, 480, LANES), np.float32)
    for a in range(OWN):
        for part in range(4):
            for b in range(OWN):
                column = 100 * part + OWN * a + b
                table[column // LANES, 48 * a + OWN * part + b, column % LANES] = 1.0
    return table


def pick_table():
    table = np.zeros((NW, 192), np.float32)
    for b in range(NW):
        slab, within = b // SLAB, b % SLAB
        table[b, 48 * (within // 20) + 20 * slab + within % 20] = 1.0
    return table


def on_device(pair_integrals, amplitudes, vir_irrep, occ_irrep, pair_irrep, vir_energy, occ_energy):
    occ = lax.axis_index("occ")
    vir = lax.axis_index("vir")

    labels_vir = vir_irrep.reshape(-1)
    own_labels = lax.dynamic_slice_in_dim(labels_vir, vir * OWN, OWN)
    own_energy = lax.dynamic_slice_in_dim(vir_energy, vir * OWN, OWN)
    label_ab = jnp.bitwise_xor(own_labels[:, None], labels_vir[None, :])
    occ_pair = occ * PAIRS + jnp.arange(PAIRS, dtype=jnp.int32)
    first_occ = occ_pair // NOCC
    second_occ = occ_pair % NOCC
    label_ij = jnp.bitwise_xor(lookup(first_occ, occ_irrep), lookup(second_occ, occ_irrep))[None, :]
    energy_ij = (lookup(first_occ, occ_energy) + lookup(second_occ, occ_energy))[None, :]
    slot = ((first_occ - (occ * PAIRS) // NOCC) * 50 + second_occ % 50)[None, :]

    label_rows = lax.dynamic_slice_in_dim(pair_irrep, vir * 96, 96)[:, None]
    packed_amp = call(
        pack_columns, jax.ShapeDtypeStruct((1, 96, SLOTS), BF16), (amplitudes, label_rows, label_ij, slot)
    )

    from_chip = lambda array, k: lax.ppermute(array, "vir", [(i, (i - 2 * k) % 16) for i in range(16)])

    turned = call(turn_rows, jax.ShapeDtypeStruct((32, CDS // 2, LANES), BF16), (pair_integrals,))
    slices = lax.all_to_all(turned, "occ", split_axis=0, concat_axis=0, tiled=True)
    blocks = call(by_partner, jax.ShapeDtypeStruct((16, CDS, LANES), BF16), (slices,))
    blocks, packed_amp = lax.optimization_barrier((blocks, packed_amp))
    amp_pair = jnp.concatenate([packed_amp, from_chip(packed_amp, 1)], axis=0)
    mirror = lax.all_to_all(blocks, "vir", split_axis=0, concat_axis=0, tiled=True)
    block_labels = label_ab.reshape(OWN, 16, OWN).transpose(1, 0, 2).reshape(16, OWN * OWN)
    block_labels = jnp.pad(block_labels, ((0, 0), (0, LANES - OWN * OWN)), constant_values=-1)
    label_cds = lax.dynamic_slice_in_dim(pair_irrep, occ * CDS, CDS)[:, None]
    copies = call(
        difference,
        jax.ShapeDtypeStruct((32, 152, LANES), BF16),
        (blocks, mirror, jnp.asarray(swap_table(), BF16), block_labels, label_cds),
    )
    copies, amp_pair = lax.optimization_barrier((copies, amp_pair))
    amp_above = from_chip(amp_pair, 2)
    amp_six = jnp.concatenate([amp_pair, amp_above, from_chip(amp_pair, 6)], axis=0)
    from_core = lambda array: lax.ppermute(array, "vir", [(i, i ^ 1) for i in range(16)])
    amp_last, core_six = lax.optimization_barrier((from_chip(amp_above, 2), from_core(amp_six)))
    amp_parts = (amp_six, core_six, amp_last, from_core(amp_last))
    gathered = lax.all_to_all(copies, "occ", split_axis=0, concat_axis=0, tiled=True)

    spread_labels = jnp.pad(
        labels_vir.reshape(2, 4, 20).transpose(1, 0, 2).reshape(4, 40), ((0, 0), (0, 8)), constant_values=-1
    ).reshape(192, 1)
    whole = lambda *shape: pl.BlockSpec(shape, lambda i: (0,) * len(shape))
    scalars = pl.BlockSpec(memory_space=pltpu.SMEM)
    return pl.pallas_call(
        finish,
        grid=(OWN // STEP,),
        out_shape=jax.ShapeDtypeStruct((OWN * NW, PAIRS), BF16),
        in_specs=[
            whole(32, 152, LANES),
            whole(4, 480, LANES),
            whole(6, 96, SLOTS),
            whole(6, 96, SLOTS),
            whole(2, 96, SLOTS),
            whole(2, 96, SLOTS),
            whole(NW, 192),
            scalars,
            scalars,
            scalars,
            whole(NW, 1),
            whole(192, 1),
            whole(NW, 1),
            whole(1, CD),
            whole(1, PAIRS),
            whole(1, PAIRS),
            whole(1, PAIRS),
        ],
        out_specs=pl.BlockSpec((STEP * NW, PAIRS), lambda i: (i, 0)),
        scratch_shapes=[
            pltpu.VMEM((CD, LANES), BF16),
            pltpu.VMEM((480, CD), BF16),
            pltpu.VMEM((CD, SLOTS), BF16),
            pltpu.VMEM((SLOTS, PAIRS), BF16),
            pltpu.VMEM((4, STEP * 192, 384), BF16),
        ],
        compiler_params=params(),
    )(
        gathered,
        jnp.asarray(place_table(), BF16),
        *amp_parts,
        jnp.asarray(pick_table(), BF16),
        vir.reshape(1),
        own_labels,
        own_energy,
        labels_vir[:, None],
        spread_labels,
        vir_energy[:, None],
        pair_irrep[None, :],
        label_ij,
        energy_ij,
        slot,
    )


def solution(mesh):
    in_specs = (P(("vir", "occ"), None), P("vir", "occ"), P(), P(), P(), P(), P())
    out_specs = P("vir", "occ")
    return jax.shard_map(
        on_device, mesh=mesh, in_specs=in_specs, out_specs=out_specs, check_vma=False
    )
```
